512 devices in a mesh: dp: 16 (over z), expert: 32 (over y, x, core).
Axes of the slice: x: 4, y: 4, z: 16, core: 2. Of those that a mesh axis runs over, the one named last changes fastest.
Arguments:
- tokens: bfloat16 [65536, 1024], P(('dp', 'expert')), may hold values from -6 to 6
- grad_out: bfloat16 [65536, 1024], P(('dp', 'expert')), may hold values from -6 to 6
- expert_ids: int32 [65536, 2], P(('dp', 'expert')), may hold values from 0 to 31, all different within a row; in each aligned block of 128 rows (0 to 127, 128 to 255, ...) at most 16 rows name the same one
- route_probs: bfloat16 [65536, 2], P(('dp', 'expert')), may hold values from 0.19921875 to 1
- gate_up_weight: bfloat16 [1024, 32, 1536], P('dp', 'expert'), may hold values from -0.1875 to 0.1875
- down_weight: bfloat16 [32, 768, 1024], P('expert'), may hold values from -0.21875 to 0.21875
- gate_up_scale_index: int32 [8, 32, 2], P(None, 'expert'), may hold values from 0 to 15
- down_scale_index: int32 [32, 6], P('expert'), may hold values from 0 to 15
- scale_table: float32 [16], replicated, may hold values from 0.5 to 2
Outputs:
- token_grad: bfloat16 [65536, 1024], P(('dp', 'expert'))
- prob_grad: float32 [65536, 2], P(('dp', 'expert'))
- gate_up_grad: bfloat16 [1024, 32, 1536], P('dp', 'expert')
- down_grad: bfloat16 [32, 768, 1024], P('expert')
The draws below stay inside these ranges and needn't reach their ends.
Inputs may be any that keep to these rules, and one draw needn't show every extreme that they name: `expert_ids`: each row names two different experts. The 128 rows of one device name one expert at most 16 times, and in every draw some device's rows name some expert exactly 16 times.
All inputs are finite; a program needn't handle non-finite values.
Results may differ from the reference program's by a relative error of at most 0.022.
Values may be sent and summed in bfloat16 or wider, within the bound.
No kernel may reach another device: no remote copies, remote signals or barrier semaphores. Data moves between devices by JAX's collectives and lax.ppermute only.
A program may use at most 64 MiB of HBM per device.

```python
import math
import jax
import jax.numpy as jnp
import numpy as np
from jax import lax

D = 1024
FF = 768
TOK_DEV = 128
QBLOCK = 128
LEVELS = 16
EXPERTS = 32
CAP = 16
TOKENS = 65536
N_DP = 16
N_EXPERT = 32


def place_ends(array, stream_key, low, high):
    longest = array.shape.index(max(array.shape))
    spots = []
    for shift in (0, 1):
        where = [jax.random.randint(jax.random.fold_in(stream_key, axis), (), 0, length) for axis, length in enumerate(array.shape)]
        where[longest] = (where[longest] + shift) % array.shape[longest]
        spots.append(tuple(where))
    return array.at[spots[0]].set(low).at[spots[1]].set(high)


def shard_levels(rng, extent, shards, smallest, largest):
    loudness = 1.0
    for dim, parts in shards:
        heights = jax.random.uniform(jax.random.fold_in(jax.random.fold_in(rng, 6), dim), (parts,), jnp.float32, smallest / len(shards), largest / len(shards))
        loudness = loudness * jnp.repeat(jnp.exp(heights), extent[dim] // parts).reshape((-1,) + (1,) * (len(extent) - 1 - dim))
    return loudness


def deal_out(own_key, own, number, rows, amount, top, reach, slope):
    order = jax.random.permutation(own_key, amount)
    packed, ordinary = portions_of(amount, rows * top, reach, slope, True), portions_of(amount, rows * top, reach, slope, False)
    places = jnp.arange(amount)

    def named(tallies, rotation):
        used = int((tallies > 0).sum())
        fixed = max(1, used // 4)
        passed = fixed + (places - fixed + rotation * (used - fixed)) % max(1, amount - fixed)
        return jnp.zeros((amount,), jnp.int32).at[order[jnp.where(places < fixed, places, passed)]].set(jnp.asarray(tallies, jnp.int32))

    tallies = jnp.where(number % 4 == 0, named(packed, number // 4), named(ordinary, number - number // 4 - 1))
    mixed = jax.random.permutation(jax.random.fold_in(own, 3), amount)
    giver, sink = mixed[0:amount // 2 * 2:2], mixed[1:amount // 2 * 2:2]
    slack = jnp.minimum(tallies[giver] - 1, reach - tallies[sink]) // 2
    slack = jnp.where((giver == order[0]) | (sink == order[0]) | (tallies[sink] == 0), 0, jnp.maximum(slack, 0))
    passed = jax.random.randint(jax.random.fold_in(own, 4), (amount // 2,), 0, 1 << 20) % (slack + 1)
    tallies = tallies.at[giver].add(-passed).at[sink].add(passed)
    labels = jnp.searchsorted(jnp.cumsum(tallies), jnp.arange(rows * top), side="right").astype(jnp.int32)
    table = labels.reshape(top, rows).T
    table = table[jax.random.permutation(jax.random.fold_in(own, 1), rows)]
    rotation = jax.random.randint(jax.random.fold_in(own, 2), (rows, 1), 0, top)
    return jnp.take_along_axis(table, (jnp.arange(top)[None, :] + rotation) % top, axis=1)


def portions_of(amount, total, reach, lean, full):
    loads = [(1 << 20) // math.isqrt(standing ** lean) + 1 for standing in range(1, amount + 1)]
    largest = reach if full else min(reach, max(-(-total // amount), total * loads[0] // sum(loads)))
    least = 1 if total - largest >= amount - 1 else 0
    given, surplus = [largest] + [least] * (amount - 1), total - largest - least * (amount - 1)
    while surplus > 0:
        free = [i for i in range(1, amount) if given[i] < largest] or [i for i in range(1, amount) if given[i] < reach]
        pool, left = sum([loads[i] for i in free]), surplus
        for i in free:
            addition = min(reach - given[i], max(1, left * loads[i] // pool), surplus)
            given[i] = given[i] + addition
            surplus = surplus - addition
    return np.array(given)


def normal_values(key, shape, deviation, limit, split=(), held_as=jnp.bfloat16):
    values = jax.random.normal(key, shape, jnp.float32) * deviation
    if len(split) > 0:
        values = shard_levels(key, shape, split, -0.22, 0.18) * values
    return jnp.clip(values, min=-limit, max=limit).astype(held_as)


def setup_inputs(seed: int = 0) -> dict:
    arg_keys = jax.random.split(jax.random.key(seed), 10)
    tokens = normal_values(arg_keys[0], (TOKENS, D), 1.0, 6.0, ((0, 512),))
    grad_out = normal_values(arg_keys[1], (TOKENS, D), 1.0, 6.0, ((0, 512),))
    expert_ids_keys = jax.random.split(jax.random.fold_in(arg_keys[2], 1), TOKENS // TOK_DEV)
    expert_ids_turns = jax.random.permutation(jax.random.fold_in(arg_keys[2], 3), TOKENS // TOK_DEV)
    expert_ids = jax.vmap(lambda own, number: deal_out(jax.random.fold_in(arg_keys[2], 2), own, number, TOK_DEV, EXPERTS, 2, CAP, 2))(expert_ids_keys, expert_ids_turns).reshape((TOKENS, 2))
    route_probs = jnp.clip(0.19921875 + 0.80078125 * jax.random.uniform(arg_keys[3], (TOKENS, 2), jnp.float32) ** shard_levels(arg_keys[3], (TOKENS, 2), ((0, 512),), -0.2, 0.2), 0.19921875, 1.0).astype(jnp.bfloat16)
    gate_up_weight = normal_values(arg_keys[4], (D, EXPERTS, 2 * FF), D ** -0.5, 0.1875, ((0, 16), (1, 32)))
    down_weight = normal_values(arg_keys[5], (EXPERTS, FF, D), FF ** -0.5, 0.21875, ((0, 32),))
    gate_up_scale_index = place_ends(jax.random.randint(arg_keys[6], (D // QBLOCK, EXPERTS, 2), 0, LEVELS), jax.random.fold_in(arg_keys[6], 1), 0, LEVELS - 1).astype(jnp.int32)
    down_scale_index = place_ends(jax.random.randint(arg_keys[7], (EXPERTS, FF // QBLOCK), 0, LEVELS), jax.random.fold_in(arg_keys[7], 1), 0, LEVELS - 1).astype(jnp.int32)
    scale_table = jnp.clip(jnp.exp(jax.random.uniform(arg_keys[8], (LEVELS,), jnp.float32, math.log(0.5), math.log(2.0))), 0.5, 2.0)
    return {"tokens": tokens, "grad_out": grad_out, "expert_ids": expert_ids, "route_probs": route_probs, "gate_up_weight": gate_up_weight, "down_weight": down_weight, "gate_up_scale_index": gate_up_scale_index, "down_scale_index": down_scale_index, "scale_table": scale_table}


def lookup(level_index, level_table):
    onehot = (level_index[..., None] == jnp.arange(level_table.shape[0], dtype=jnp.int32)).astype(level_table.dtype)
    return jnp.sum(onehot * level_table, axis=-1)


def slot_tables(routes, experts, capacity):
    flat_routes = routes.reshape(-1)
    expert_hits = (flat_routes[:, None] == jnp.arange(experts, dtype=jnp.int32)[None, :]).astype(jnp.int32)
    before = jnp.cumsum(expert_hits, axis=0) - expert_hits
    slot_rank = jnp.sum(before * expert_hits, axis=1)
    destination = flat_routes * capacity + slot_rank
    table_hits = destination[:, None] == jnp.arange(experts * capacity, dtype=jnp.int32)[None, :]
    return table_hits.astype(jnp.float32).reshape(routes.shape[0], 2, experts * capacity)


def reference(tokens, grad_out, expert_ids, route_probs, gate_up_weight, down_weight, gate_up_scale_index, down_scale_index, scale_table):
    high = lax.Precision.HIGHEST
    f32 = jnp.float32
    slots_all = EXPERTS * CAP
    level_rows = jnp.repeat(lookup(gate_up_scale_index, scale_table), QBLOCK, axis=0)
    full_scale = jnp.repeat(level_rows, FF, axis=2)
    down_scale = jnp.repeat(lookup(down_scale_index, scale_table), QBLOCK, axis=1)
    gate_up_eff = (gate_up_weight.astype(f32) * full_scale).astype(jnp.bfloat16)
    down_eff = (down_weight.astype(f32) * down_scale[:, :, None]).astype(jnp.bfloat16)
    gate_up_wide = gate_up_eff.astype(f32)
    down_wide = down_eff.astype(f32)
    grid = (N_DP, N_EXPERT, TOK_DEV)
    inputs = (tokens.reshape(grid + (D,)), grad_out.reshape(grid + (D,)),
              expert_ids.reshape(grid + (2,)), route_probs.reshape(grid + (2,)))

    def row_step(totals, pieces):
        rows_in, grads_in, routes, probs = pieces
        slot_hits = jax.vmap(lambda r: slot_tables(r, EXPERTS, CAP))(routes)
        either = slot_hits[:, :, 0] + slot_hits[:, :, 1]
        row_shape = (N_EXPERT, EXPERTS, CAP, D)
        recv_tokens = jnp.einsum("ats,atd->asd", either, rows_in.astype(f32)).astype(jnp.bfloat16).reshape(row_shape)
        recv_grads = jnp.einsum("ats,atd->asd", either, grads_in.astype(f32)).astype(jnp.bfloat16).reshape(row_shape)
        recv_probs = jnp.einsum("atks,atk->as", slot_hits, probs.astype(f32), precision=high).reshape(row_shape[:3])
        projected = jnp.einsum("sjcd,djf->sjcf", recv_tokens.astype(f32), gate_up_wide)
        gate_part = projected[..., :FF]
        up_part = projected[..., FF:]
        sigmoid_gate = jax.nn.sigmoid(gate_part)
        activated = gate_part * sigmoid_gate
        hidden_rows = (activated * up_part).astype(jnp.bfloat16)
        hidden_grad = jnp.einsum("sjcd,jfd->sjcf", recv_grads.astype(f32), down_wide)
        scaled_grad = recv_probs[..., None] * hidden_grad
        gate_grad = scaled_grad * up_part * sigmoid_gate * (1.0 + gate_part * (1.0 - sigmoid_gate))
        up_grad = scaled_grad * activated
        joint_grad = jnp.concatenate([gate_grad, up_grad], axis=-1).astype(jnp.bfloat16)
        row_grads = jnp.einsum("sjcf,djf->sjcd", joint_grad.astype(f32), gate_up_wide).astype(jnp.bfloat16)
        token_part = jnp.einsum("ats,asd->atd", either, row_grads.reshape(N_EXPERT, slots_all, D).astype(f32)).astype(jnp.bfloat16)
        expert_out = jnp.einsum("sjcf,jfd->sjcd", hidden_rows.astype(f32), down_wide)
        picked = jnp.einsum("atks,asd->atkd", slot_hits, expert_out.reshape(N_EXPERT, slots_all, D), precision=high)
        prob_part = jnp.sum(picked * grads_in.astype(f32)[:, :, None, :], axis=-1)
        weighted = (recv_probs[..., None] * hidden_rows.astype(f32)).astype(jnp.bfloat16)
        gate_up_part = (jnp.einsum("sjcd,sjcf->djf", recv_tokens.astype(f32), joint_grad.astype(f32)) * full_scale).astype(jnp.bfloat16)
        down_part = (jnp.einsum("sjcf,sjcd->jfd", weighted.astype(f32), recv_grads.astype(f32)) * down_scale[:, :, None]).astype(jnp.bfloat16)
        totals = (totals[0] + gate_up_part.astype(f32), totals[1] + down_part.astype(f32))
        return totals, (token_part, prob_part)

    start_sums = (jnp.zeros((D, EXPERTS, 2 * FF), f32), jnp.zeros((EXPERTS, FF, D), f32))
    sums, outputs = lax.scan(row_step, start_sums, inputs)
    token_grad = outputs[0].reshape(TOKENS, D)
    prob_grad = outputs[1].reshape(TOKENS, 2)
    return token_grad, prob_grad, sums[0].astype(jnp.bfloat16), sums[1].astype(jnp.bfloat16)
```

```python
import jax
import jax.numpy as jnp
from jax import lax
from jax.sharding import PartitionSpec as P

QBLOCK = 128


def lookup(level_index, level_table):
    onehot = (level_index[..., None] == jnp.arange(level_table.shape[0], dtype=jnp.int32)).astype(
        level_table.dtype
    )
    return jnp.sum(onehot * level_table, axis=-1)


def slot_tables(routes, experts, capacity):
    flat_routes = routes.reshape(-1)
    expert_hits = (flat_routes[:, None] == jnp.arange(experts, dtype=jnp.int32)[None, :]).astype(
        jnp.int32
    )
    place = jnp.arange(flat_routes.shape[0], dtype=jnp.int32)
    earlier = (place[None, :] < place[:, None]).astype(jnp.bfloat16)
    before = jnp.dot(
        earlier, expert_hits.astype(jnp.bfloat16), preferred_element_type=jnp.float32
    ).astype(jnp.int32)
    slot_rank = jnp.sum(before * expert_hits, axis=1)
    destination = flat_routes * capacity + slot_rank
    table_hits = destination[:, None] == jnp.arange(experts * capacity, dtype=jnp.int32)[None, :]
    return table_hits.astype(jnp.float32).reshape(routes.shape[0], 2, experts * capacity)


def body(
    tokens,
    grad_out,
    expert_ids,
    route_probs,
    gate_up_weight,
    down_weight,
    gate_up_scale_index,
    down_scale_index,
    scale_table,
):
    high = lax.Precision.HIGHEST
    f32 = jnp.float32
    groups = lax.axis_size("expert")
    tok_dev = tokens.shape[0]
    model_width = tokens.shape[1]
    per_device = down_weight.shape[0]
    hidden = down_weight.shape[1]
    experts = per_device * groups
    capacity = 4 * tok_dev // experts
    slots_all = experts * capacity
    slot_hits = slot_tables(expert_ids, experts, capacity)
    either = (slot_hits[:, 0] + slot_hits[:, 1]).astype(jnp.bfloat16)
    row_shape = (groups, per_device, capacity, model_width)
    send_tokens = (
        jnp.einsum("ts,td->sd", either, tokens, preferred_element_type=f32)
        .astype(jnp.bfloat16)
        .reshape(row_shape)
    )
    send_grads = (
        jnp.einsum("ts,td->sd", either, grad_out, preferred_element_type=f32)
        .astype(jnp.bfloat16)
        .reshape(row_shape)
    )
    send_probs = (
        jnp.einsum("tks,tk->s", slot_hits, route_probs.astype(f32), precision=high)
        .astype(jnp.bfloat16)
        .reshape(row_shape[:3])
    )
    recv_tokens, recv_grads, recv_probs = (
        lax.all_to_all(send_tokens, "expert", split_axis=0, concat_axis=0, tiled=True),
        lax.all_to_all(send_grads, "expert", split_axis=0, concat_axis=0, tiled=True),
        lax.all_to_all(send_probs, "expert", split_axis=0, concat_axis=0, tiled=True),
    )
    level_rows = jnp.repeat(lookup(gate_up_scale_index, scale_table), QBLOCK, axis=0)
    full_scale = jnp.repeat(level_rows, hidden, axis=2)
    down_scale = jnp.repeat(lookup(down_scale_index, scale_table), QBLOCK, axis=1)
    down_eff = (down_weight.astype(f32) * down_scale[:, :, None]).astype(jnp.bfloat16)
    gathered = lax.all_gather(gate_up_weight, "dp", axis=0, tiled=True)
    gate_up_eff = (gathered.astype(f32) * full_scale).astype(jnp.bfloat16)
    projected = jnp.einsum("sjcd,djf->sjcf", recv_tokens, gate_up_eff, preferred_element_type=f32)
    gate_part = projected[..., :hidden]
    up_part = projected[..., hidden:]
    sigmoid_gate = jax.nn.sigmoid(gate_part)
    activated = gate_part * sigmoid_gate
    hidden_rows = (activated * up_part).astype(jnp.bfloat16)
    hidden_grad = jnp.einsum("sjcd,jfd->sjcf", recv_grads, down_eff, preferred_element_type=f32)
    probs_wide = recv_probs.astype(f32)[..., None]
    scaled_grad = probs_wide * hidden_grad
    gate_grad = scaled_grad * up_part * sigmoid_gate * (1.0 + gate_part * (1.0 - sigmoid_gate))
    up_grad = scaled_grad * activated
    joint_grad = jnp.concatenate([gate_grad, up_grad], axis=-1).astype(jnp.bfloat16)
    row_grads = jnp.einsum(
        "sjcf,djf->sjcd", joint_grad, gate_up_eff, preferred_element_type=f32
    ).astype(jnp.bfloat16)
    back_rows = lax.all_to_all(row_grads, "expert", split_axis=0, concat_axis=0, tiled=True)
    token_grad = jnp.dot(
        either, back_rows.reshape(slots_all, model_width), preferred_element_type=f32
    ).astype(jnp.bfloat16)
    expert_out = jnp.einsum("sjcf,jfd->sjcd", hidden_rows, down_eff, preferred_element_type=f32)
    back_out = lax.all_to_all(
        expert_out.astype(jnp.bfloat16), "expert", split_axis=0, concat_axis=0, tiled=True
    ).astype(expert_out.dtype)
    picked = jnp.einsum(
        "tks,sd->tkd", slot_hits, back_out.reshape(slots_all, model_width), precision=high
    )
    prob_grad = jnp.sum(picked * grad_out.astype(f32)[:, None, :], axis=-1)
    weighted = (probs_wide * hidden_rows.astype(f32)).astype(jnp.bfloat16)
    partial_sum = jnp.einsum("sjcd,sjcf->djf", recv_tokens, joint_grad, preferred_element_type=f32)
    gate_up_grad = lax.psum_scatter(
        (partial_sum * full_scale).astype(jnp.bfloat16), "dp", scatter_dimension=0, tiled=True
    )
    down_part = (
        jnp.einsum("sjcf,sjcd->jfd", weighted, recv_grads, preferred_element_type=f32)
        * down_scale[:, :, None]
    )
    down_grad = lax.psum(down_part.astype(jnp.bfloat16), "dp")
    return (token_grad, prob_grad, gate_up_grad, down_grad)


def solution(mesh):
    in_specs = (
        P(("dp", "expert"), None),
        P(("dp", "expert"), None),
        P(("dp", "expert"), None),
        P(("dp", "expert"), None),
        P("dp", "expert", None),
        P("expert", None, None),
        P(None, "expert", None),
        P("expert", None),
        P(),
    )
    out_specs = (
        P(("dp", "expert"), None),
        P(("dp", "expert"), None),
        P("dp", "expert", None),
        P("expert", None, None),
    )
    return jax.shard_map(body, mesh=mesh, in_specs=in_specs, out_specs=out_specs, check_vma=False)
```

```python
import jax
import jax.numpy as jnp
from jax import lax
from jax.experimental import pallas as pl
from jax.experimental.pallas import tpu as pltpu
from jax.sharding import PartitionSpec as P

QBLOCK = 128
LANES = 128
FTILE = 256
bf16 = jnp.bfloat16
f32 = jnp.float32


def lookup(level_index, level_table):
    onehot = (level_index[..., None] == jnp.arange(level_table.shape[0], dtype=jnp.int32)).astype(
        level_table.dtype
    )
    return jnp.sum(onehot * level_table, axis=-1)


def slot_tables(routes, experts, capacity):
    flat_routes = routes.reshape(-1)
    expert_hits = (flat_routes[:, None] == jnp.arange(experts, dtype=jnp.int32)[None, :]).astype(
        jnp.int32
    )
    place = jnp.arange(flat_routes.shape[0], dtype=jnp.int32)
    earlier = (place[None, :] < place[:, None]).astype(bf16)
    before = jnp.dot(earlier, expert_hits.astype(bf16), preferred_element_type=f32).astype(
        jnp.int32
    )
    slot_rank = jnp.sum(before * expert_hits, axis=1)
    destination = flat_routes * capacity + slot_rank
    table_hits = destination[:, None] == jnp.arange(experts * capacity, dtype=jnp.int32)[None, :]
    return table_hits.astype(f32).reshape(routes.shape[0], 2, experts * capacity)


def scaled_rows(w_ref, scale_ref, part):
    blocks = w_ref.shape[0] // QBLOCK
    pieces = [
        (w_ref[QBLOCK * b : QBLOCK * (b + 1), :].astype(f32) * scale_ref[b, part]).astype(bf16)
        for b in range(blocks)
    ]
    return jnp.concatenate(pieces, axis=0)


def hidden_kernel(
    gu_scale, d_scale, x_ref, xt_ref, g_ref, hg_ref, wg_ref, wu_ref, sums_ref, joint_ref, dots_ref
):
    step = pl.program_id(0)
    x = x_ref[...]
    gate = jnp.dot(x, scaled_rows(wg_ref, gu_scale, 0), preferred_element_type=f32)
    up = jnp.dot(x, scaled_rows(wu_ref, gu_scale, 1), preferred_element_type=f32)
    sig = jax.nn.sigmoid(gate)
    act = gate * sig
    hidden = (act * up).astype(bf16)
    hg = hg_ref[...]
    joint = (
        (hg * up * sig * (1.0 + gate * (1.0 - sig))).astype(bf16),
        (hg * act).astype(bf16),
    )
    dots = jnp.sum(hidden.astype(f32) * hg, axis=1, keepdims=True)

    @pl.when(step == 0)
    def _():
        dots_ref[...] = dots

    @pl.when(step > 0)
    def _():
        dots_ref[...] += dots

    owners = sums_ref.shape[0]
    rows = xt_ref.shape[0] // owners
    xt = xt_ref[...]
    for k in range(2):
        joint_ref[k] = joint[k]
        part = jnp.dot(xt, joint[k], preferred_element_type=f32)
        for r in range(owners):
            piece = part[rows * r : rows * (r + 1), :] * gu_scale[rows * r // QBLOCK, k]
            for c in range(FTILE // LANES):
                at = (2 * k + c) * rows
                sums_ref[r, at : at + rows, :] = piece[:, LANES * c : LANES * (c + 1)].astype(bf16)
    part = lax.dot_general(
        hidden, g_ref[...], (((0,), (0,)), ((), ())), preferred_element_type=f32
    )
    drows = FTILE // owners
    base = 2 * (FTILE // LANES) * rows
    for r in range(owners):
        piece = part[drows * r : drows * (r + 1), :] * d_scale[
            step * (FTILE // QBLOCK) + drows * r // QBLOCK
        ]
        for c in range(part.shape[1] // LANES):
            at = base + c * drows
            sums_ref[r, at : at + drows, :] = piece[:, LANES * c : LANES * (c + 1)].astype(bf16)


def hidden_step(gu_scale, d_scale, x, xt, g, hg, weights, owners):
    slots, width = x.shape
    hidden = hg.shape[1]
    steps = hidden // FTILE
    rows = width // owners
    per_step = 2 * (FTILE // LANES) * rows + (FTILE // owners) * (width // LANES)
    smem = pl.BlockSpec(memory_space=pltpu.SMEM)
    whole = lambda a: pl.BlockSpec(a.shape, lambda i: (0, 0))
    flops = 2 * slots * width * hidden * 5
    return pl.pallas_call(
        hidden_kernel,
        grid=(steps,),
        in_specs=[
            smem,
            smem,
            whole(x),
            whole(xt),
            whole(g),
            pl.BlockSpec((slots, FTILE), lambda i: (0, i)),
            pl.BlockSpec((width, FTILE), lambda i: (0, i)),
            pl.BlockSpec((width, FTILE), lambda i, n=steps: (0, n + i)),
        ],
        out_specs=[
            pl.BlockSpec((owners, per_step, LANES), lambda i: (0, i, 0)),
            pl.BlockSpec((2, slots, FTILE), lambda i: (0, 0, i)),
            pl.BlockSpec((slots, 1), lambda i: (0, 0)),
        ],
        out_shape=[
            jax.ShapeDtypeStruct((owners, per_step * steps, LANES), bf16),
            jax.ShapeDtypeStruct((2, slots, hidden), bf16),
            jax.ShapeDtypeStruct((slots, 1), f32),
        ],
        compiler_params=pltpu.CompilerParams(vmem_limit_bytes=48 * 1024 * 1024),
        cost_estimate=pl.CostEstimate(
            flops=flops, bytes_accessed=14 * 1024 * 1024, transcendentals=slots * hidden
        ),
    )(gu_scale, d_scale, x, xt, g, hg, weights, weights)


def rows_kernel(gu_scale, joint_ref, wg_ref, wu_ref, out_ref, total):
    step = pl.program_id(0)
    contract = (((1,), (1,)), ((), ()))
    part = lax.dot_general(
        joint_ref[0], scaled_rows(wg_ref, gu_scale, 0), contract, preferred_element_type=f32
    ) + lax.dot_general(
        joint_ref[1], scaled_rows(wu_ref, gu_scale, 1), contract, preferred_element_type=f32
    )

    @pl.when(step == 0)
    def _():
        total[...] = part

    @pl.when(step > 0)
    def _():
        total[...] += part

    @pl.when(step == pl.num_programs(0) - 1)
    def _():
        out_ref[...] = total[...].astype(bf16)


def rows_step(gu_scale, joint, weights):
    slots, hidden = joint.shape[1:]
    width = weights.shape[0]
    steps = hidden // FTILE
    return pl.pallas_call(
        rows_kernel,
        grid=(steps,),
        in_specs=[
            pl.BlockSpec(memory_space=pltpu.SMEM),
            pl.BlockSpec((2, slots, FTILE), lambda i: (0, 0, i)),
            pl.BlockSpec((width, FTILE), lambda i: (0, i)),
            pl.BlockSpec((width, FTILE), lambda i, n=steps: (0, n + i)),
        ],
        out_specs=pl.BlockSpec((slots, width), lambda i: (0, 0)),
        out_shape=jax.ShapeDtypeStruct((slots, width), bf16),
        scratch_shapes=[pltpu.VMEM((slots, width), f32)],
        compiler_params=pltpu.CompilerParams(vmem_limit_bytes=32 * 1024 * 1024),
        cost_estimate=pl.CostEstimate(
            flops=4 * slots * width * hidden, bytes_accessed=6 * 1024 * 1024, transcendentals=0
        ),
    )(gu_scale, joint, weights, weights)


def body(
    tokens,
    grad_out,
    expert_ids,
    route_probs,
    gate_up_weight,
    down_weight,
    gate_up_scale_index,
    down_scale_index,
    scale_table,
):
    groups = lax.axis_size("expert")
    owners = lax.axis_size("dp")
    tok_dev, width = tokens.shape
    hidden = down_weight.shape[1]
    capacity = 4 * tok_dev // groups
    slots = groups * capacity
    steps = hidden // FTILE

    gathered = lax.all_gather(
        gate_up_weight.reshape(gate_up_weight.shape[0], 2 * hidden), "dp", axis=0, tiled=True
    )

    slot_hits = slot_tables(expert_ids, groups, capacity)
    either = (slot_hits[:, 0] + slot_hits[:, 1]).astype(bf16)
    weighing = jnp.sum(slot_hits * route_probs.astype(f32)[:, :, None], axis=1).astype(bf16)
    pack = lambda table, values: (
        jnp.einsum("ts,td->sd", table, values, preferred_element_type=f32)
        .astype(bf16)
        .reshape(groups, capacity, width)
    )
    send = jnp.concatenate([pack(either, tokens), pack(weighing, grad_out)], axis=1)
    recv = lax.all_to_all(send, "expert", split_axis=0, concat_axis=0, tiled=True)
    x = recv[:, :capacity].reshape(slots, width)
    g = recv[:, capacity:].reshape(slots, width)
    xt = x.T
    gu_scale = lookup(gate_up_scale_index[:, 0, :], scale_table)
    d_scale = lookup(down_scale_index[0], scale_table)
    down_eff = (
        down_weight[0].astype(f32) * jnp.repeat(d_scale, QBLOCK)[:, None]
    ).astype(bf16)
    hg = jnp.einsum("sd,fd->sf", g, down_eff, preferred_element_type=f32)

    sums, joint, dots = hidden_step(gu_scale, d_scale, x, xt, g, hg, gathered, owners)
    mine = lax.psum_scatter(sums, "dp", scatter_dimension=0, tiled=True)
    row_grads = rows_step(gu_scale, joint, gathered).reshape(groups, capacity, width)
    back_rows = lax.all_to_all(row_grads, "expert", split_axis=0, concat_axis=0, tiled=True)
    back_dots = lax.all_to_all(
        dots.reshape(groups, capacity), "expert", split_axis=0, concat_axis=0, tiled=True
    )
    token_grad = jnp.dot(
        either, back_rows.reshape(slots, width), preferred_element_type=f32
    ).astype(bf16)
    prob_grad = jnp.sum(slot_hits * back_dots.reshape(slots), axis=-1) / route_probs.astype(f32)

    rows = width // owners
    tiles = FTILE // LANES
    mine = mine.reshape(steps, -1, LANES)
    cut = 2 * tiles * rows
    gate_up_grad = (
        mine[:, :cut]
        .reshape(steps, 2, tiles, rows, LANES)
        .transpose(3, 1, 0, 2, 4)
        .reshape(rows, 1, 2 * hidden)
    )
    drows = FTILE // owners
    shared = lax.all_gather(
        mine[:, cut:].reshape(-1, LANES), "dp", axis=0, tiled=True
    ).reshape(owners, steps, width // LANES, drows, LANES)
    down_grad = shared.transpose(1, 0, 3, 2, 4).reshape(1, hidden, width)
    return (token_grad, prob_grad, gate_up_grad, down_grad)


def solution(mesh):
    in_specs = (
        P(("dp", "expert"), None),
        P(("dp", "expert"), None),
        P(("dp", "expert"), None),
        P(("dp", "expert"), None),
        P("dp", "expert", None),
        P("expert", None, None),
        P(None, "expert", None),
        P("expert", None),
        P(),
    )
    out_specs = (
        P(("dp", "expert"), None),
        P(("dp", "expert"), None),
        P("dp", "expert", None),
        P("expert", None, None),
    )
    return jax.shard_map(body, mesh=mesh, in_specs=in_specs, out_specs=out_specs, check_vma=False)
```

```python
import jax
import jax.numpy as jnp
from jax import lax
from jax.experimental import pallas as pl
from jax.experimental.pallas import tpu as pltpu
from jax.sharding import PartitionSpec as P

QBLOCK = 128
LANES = 128
FTILE = 256
bf16 = jnp.bfloat16
f32 = jnp.float32


def lookup(level_index, level_table):
    onehot = (level_index[..., None] == jnp.arange(level_table.shape[0], dtype=jnp.int32)).astype(
        level_table.dtype
    )
    return jnp.sum(onehot * level_table, axis=-1)


def slot_tables(routes, experts, capacity):
    flat_routes = routes.reshape(-1)
    expert_hits = (flat_routes[:, None] == jnp.arange(experts, dtype=jnp.int32)[None, :]).astype(
        jnp.int32
    )
    place = jnp.arange(flat_routes.shape[0], dtype=jnp.int32)
    earlier = (place[None, :] < place[:, None]).astype(bf16)
    before = jnp.dot(earlier, expert_hits.astype(bf16), preferred_element_type=f32).astype(
        jnp.int32
    )
    slot_rank = jnp.sum(before * expert_hits, axis=1)
    destination = flat_routes * capacity + slot_rank
    table_hits = destination[:, None] == jnp.arange(experts * capacity, dtype=jnp.int32)[None, :]
    return table_hits.astype(f32).reshape(routes.shape[0], 2, experts * capacity)


def scaled_rows(w_ref, scale_ref, part):
    blocks = w_ref.shape[0] // QBLOCK
    pieces = [
        (w_ref[QBLOCK * b : QBLOCK * (b + 1), :].astype(f32) * scale_ref[b, part]).astype(bf16)
        for b in range(blocks)
    ]
    return jnp.concatenate(pieces, axis=0)


def hidden_kernel(
    gu_scale, d_scale, x_ref, xt_ref, g_ref, hg_ref, wg_ref, wu_ref, sums_ref, joint_ref, dots_ref
):
    step = pl.program_id(0)
    x = x_ref[...]
    gate = jnp.dot(x, scaled_rows(wg_ref, gu_scale, 0), preferred_element_type=f32)
    up = jnp.dot(x, scaled_rows(wu_ref, gu_scale, 1), preferred_element_type=f32)
    sig = jax.nn.sigmoid(gate)
    act = gate * sig
    hidden = (act * up).astype(bf16)
    hg = hg_ref[...]
    joint = (
        (hg * up * sig * (1.0 + gate * (1.0 - sig))).astype(bf16),
        (hg * act).astype(bf16),
    )
    dots = jnp.sum(hidden.astype(f32) * hg, axis=1, keepdims=True)

    @pl.when(step == 0)
    def _():
        dots_ref[...] = dots

    @pl.when(step > 0)
    def _():
        dots_ref[...] += dots

    owners = sums_ref.shape[0]
    rows = xt_ref.shape[0] // owners
    xt = xt_ref[...]
    for k in range(2):
        joint_ref[k] = joint[k]
        part = jnp.dot(xt, joint[k], preferred_element_type=f32)
        for r in range(owners):
            piece = part[rows * r : rows * (r + 1), :] * gu_scale[rows * r // QBLOCK, k]
            for c in range(FTILE // LANES):
                at = (2 * k + c) * rows
                sums_ref[r, at : at + rows, :] = piece[:, LANES * c : LANES * (c + 1)].astype(bf16)
    part = lax.dot_general(
        hidden, g_ref[...], (((0,), (0,)), ((), ())), preferred_element_type=f32
    )
    drows = FTILE // owners
    base = 2 * (FTILE // LANES) * rows
    for r in range(owners):
        own = (r % 2) * (owners // 2) + r // 2
        piece = part[drows * own : drows * (own + 1), :] * d_scale[
            step * (FTILE // QBLOCK) + drows * own // QBLOCK
        ]
        for c in range(part.shape[1] // LANES):
            at = base + c * drows
            sums_ref[r, at : at + drows, :] = piece[:, LANES * c : LANES * (c + 1)].astype(bf16)


def hidden_step(gu_scale, d_scale, x, xt, g, hg, weights, owners):
    slots, width = x.shape
    hidden = hg.shape[1]
    steps = hidden // FTILE
    rows = width // owners
    per_step = 2 * (FTILE // LANES) * rows + (FTILE // owners) * (width // LANES)
    smem = pl.BlockSpec(memory_space=pltpu.SMEM)
    whole = lambda a: pl.BlockSpec(a.shape, lambda i: (0, 0))
    flops = 2 * slots * width * hidden * 5
    return pl.pallas_call(
        hidden_kernel,
        grid=(steps,),
        in_specs=[
            smem,
            smem,
            whole(x),
            whole(xt),
            whole(g),
            pl.BlockSpec((slots, FTILE), lambda i: (0, i)),
            pl.BlockSpec((width, FTILE), lambda i: (0, i)),
            pl.BlockSpec((width, FTILE), lambda i, n=steps: (0, n + i)),
        ],
        out_specs=[
            pl.BlockSpec((owners, per_step, LANES), lambda i: (0, i, 0)),
            pl.BlockSpec((2, slots, FTILE), lambda i: (0, 0, i)),
            pl.BlockSpec((slots, 1), lambda i: (0, 0)),
        ],
        out_shape=[
            jax.ShapeDtypeStruct((owners, per_step * steps, LANES), bf16),
            jax.ShapeDtypeStruct((2, slots, hidden), bf16),
            jax.ShapeDtypeStruct((slots, 1), f32),
        ],
        compiler_params=pltpu.CompilerParams(vmem_limit_bytes=48 * 1024 * 1024),
        cost_estimate=pl.CostEstimate(
            flops=flops, bytes_accessed=14 * 1024 * 1024, transcendentals=slots * hidden
        ),
    )(gu_scale, d_scale, x, xt, g, hg, weights, weights)


def rows_kernel(gu_scale, joint_ref, wg_ref, wu_ref, out_ref, total):
    step = pl.program_id(0)
    contract = (((1,), (1,)), ((), ()))
    part = lax.dot_general(
        joint_ref[0], scaled_rows(wg_ref, gu_scale, 0), contract, preferred_element_type=f32
    ) + lax.dot_general(
        joint_ref[1], scaled_rows(wu_ref, gu_scale, 1), contract, preferred_element_type=f32
    )

    @pl.when(step == 0)
    def _():
        total[...] = part

    @pl.when(step > 0)
    def _():
        total[...] += part

    @pl.when(step == pl.num_programs(0) - 1)
    def _():
        out_ref[...] = total[...].astype(bf16)


def rows_step(gu_scale, joint, weights):
    slots, hidden = joint.shape[1:]
    width = weights.shape[0]
    steps = hidden // FTILE
    return pl.pallas_call(
        rows_kernel,
        grid=(steps,),
        in_specs=[
            pl.BlockSpec(memory_space=pltpu.SMEM),
            pl.BlockSpec((2, slots, FTILE), lambda i: (0, 0, i)),
            pl.BlockSpec((width, FTILE), lambda i: (0, i)),
            pl.BlockSpec((width, FTILE), lambda i, n=steps: (0, n + i)),
        ],
        out_specs=pl.BlockSpec((slots, width), lambda i: (0, 0)),
        out_shape=jax.ShapeDtypeStruct((slots, width), bf16),
        scratch_shapes=[pltpu.VMEM((slots, width), f32)],
        compiler_params=pltpu.CompilerParams(vmem_limit_bytes=32 * 1024 * 1024),
        cost_estimate=pl.CostEstimate(
            flops=4 * slots * width * hidden, bytes_accessed=6 * 1024 * 1024, transcendentals=0
        ),
    )(gu_scale, joint, weights, weights)


def body(
    tokens,
    grad_out,
    expert_ids,
    route_probs,
    gate_up_weight,
    down_weight,
    gate_up_scale_index,
    down_scale_index,
    scale_table,
):
    groups = lax.axis_size("expert")
    owners = lax.axis_size("dp")
    tok_dev, width = tokens.shape
    hidden = down_weight.shape[1]
    capacity = 4 * tok_dev // groups
    slots = groups * capacity
    steps = hidden // FTILE

    gathered = lax.all_gather(
        gate_up_weight.reshape(gate_up_weight.shape[0], 2 * hidden), "dp", axis=0, tiled=True
    )

    slot_hits = slot_tables(expert_ids, groups, capacity)
    either = (slot_hits[:, 0] + slot_hits[:, 1]).astype(bf16)
    weighing = jnp.sum(slot_hits * route_probs.astype(f32)[:, :, None], axis=1).astype(bf16)
    pack = lambda table, values: (
        jnp.einsum("ts,td->sd", table, values, preferred_element_type=f32)
        .astype(bf16)
        .reshape(groups, capacity, width)
    )
    send = jnp.concatenate([pack(either, tokens), pack(weighing, grad_out)], axis=1)
    recv = lax.all_to_all(send, "expert", split_axis=0, concat_axis=0, tiled=True)
    x = recv[:, :capacity].reshape(slots, width)
    g = recv[:, capacity:].reshape(slots, width)
    xt = x.T
    gu_scale = lookup(gate_up_scale_index[:, 0, :], scale_table)
    d_scale = lookup(down_scale_index[0], scale_table)
    down_eff = (
        down_weight[0].astype(f32) * jnp.repeat(d_scale, QBLOCK)[:, None]
    ).astype(bf16)
    hg = jnp.einsum("sd,fd->sf", g, down_eff, preferred_element_type=f32)

    sums, joint, dots = hidden_step(gu_scale, d_scale, x, xt, g, hg, gathered, owners)
    mine = lax.psum_scatter(sums, "dp", scatter_dimension=0, tiled=True)
    row_grads = rows_step(gu_scale, joint, gathered).reshape(groups, capacity, width)
    back_rows = lax.all_to_all(row_grads, "expert", split_axis=0, concat_axis=0, tiled=True)
    back_dots = lax.all_to_all(
        dots.reshape(groups, capacity), "expert", split_axis=0, concat_axis=0, tiled=True
    )
    token_grad = jnp.dot(
        either, back_rows.reshape(slots, width), preferred_element_type=f32
    ).astype(bf16)
    prob_grad = jnp.sum(slot_hits * back_dots.reshape(slots), axis=-1) / route_probs.astype(f32)

    mine, token_grad, prob_grad = lax.optimization_barrier((mine, token_grad, prob_grad))
    rows = width // owners
    tiles = FTILE // LANES
    mine = mine.reshape(steps, -1, LANES)
    cut = 2 * tiles * rows
    gate_up_grad = (
        mine[:, :cut]
        .reshape(steps, 2, tiles, rows, LANES)
        .transpose(3, 1, 0, 2, 4)
        .reshape(rows, 1, 2 * hidden)
    )
    drows = FTILE // owners
    own = (
        mine[:, cut:]
        .reshape(steps, width // LANES, drows, LANES)
        .transpose(0, 2, 1, 3)
        .reshape(steps, drows, width)
    )
    same_parity = [list(range(k, owners, 2)) for k in range(2)]
    neighbours = [[k, k + 1] for k in range(0, owners, 2)]
    gather = lambda a, sets: lax.all_gather(
        a, "dp", axis=1, tiled=True, axis_index_groups=sets
    )
    half = gather(own, same_parity)
    down_grad = jnp.concatenate(
        [gather(half[:, :, : width // 2], neighbours), gather(half[:, :, width // 2 :], neighbours)],
        axis=2,
    ).reshape(1, hidden, width)
    return (token_grad, prob_grad, gate_up_grad, down_grad)


def solution(mesh):
    in_specs = (
        P(("dp", "expert"), None),
        P(("dp", "expert"), None),
        P(("dp", "expert"), None),
        P(("dp", "expert"), None),
        P("dp", "expert", None),
        P("expert", None, None),
        P(None, "expert", None),
        P("expert", None),
        P(),
    )
    out_specs = (
        P(("dp", "expert"), None),
        P(("dp", "expert"), None),
        P("dp", "expert", None),
        P("expert", None, None),
    )
    return jax.shard_map(body, mesh=mesh, in_specs=in_specs, out_specs=out_specs, check_vma=False)
```

```python
import jax
import jax.numpy as jnp
from jax import lax
from jax.experimental import pallas as pl
from jax.experimental.pallas import tpu as pltpu
from jax.sharding import PartitionSpec as P

QBLOCK = 128
LANES = 128
FTILE = 256
EARLY = 3
bf16 = jnp.bfloat16
f32 = jnp.float32


def lookup(level_index, level_table):
    onehot = (level_index[..., None] == jnp.arange(level_table.shape[0], dtype=jnp.int32)).astype(
        level_table.dtype
    )
    return jnp.sum(onehot * level_table, axis=-1)


def slot_tables(routes, experts, capacity):
    flat_routes = routes.reshape(-1)
    expert_hits = (flat_routes[:, None] == jnp.arange(experts, dtype=jnp.int32)[None, :]).astype(
        jnp.int32
    )
    place = jnp.arange(flat_routes.shape[0], dtype=jnp.int32)
    earlier = (place[None, :] < place[:, None]).astype(bf16)
    before = jnp.dot(earlier, expert_hits.astype(bf16), preferred_element_type=f32).astype(
        jnp.int32
    )
    slot_rank = jnp.sum(before * expert_hits, axis=1)
    destination = flat_routes * capacity + slot_rank
    table_hits = destination[:, None] == jnp.arange(experts * capacity, dtype=jnp.int32)[None, :]
    return table_hits.astype(f32).reshape(routes.shape[0], 2, experts * capacity)


def scaled_rows(w_ref, scale_ref, part):
    blocks = w_ref.shape[0] // QBLOCK
    pieces = [
        (w_ref[QBLOCK * b : QBLOCK * (b + 1), :].astype(f32) * scale_ref[b, part]).astype(bf16)
        for b in range(blocks)
    ]
    return jnp.concatenate(pieces, axis=0)


def hidden_kernel(
    gu_scale, d_scale, x_ref, xt_ref, g_ref, hg_ref, wg_ref, wu_ref, sums_ref, early_ref, joint_ref, dots_ref
):
    step = pl.program_id(0)
    x = x_ref[...]
    gate = jnp.dot(x, scaled_rows(wg_ref, gu_scale, 0), preferred_element_type=f32)
    up = jnp.dot(x, scaled_rows(wu_ref, gu_scale, 1), preferred_element_type=f32)
    sig = jax.nn.sigmoid(gate)
    act = gate * sig
    hidden = (act * up).astype(bf16)
    hg = hg_ref[...]
    joint = (
        (hg * up * sig * (1.0 + gate * (1.0 - sig))).astype(bf16),
        (hg * act).astype(bf16),
    )
    dots = jnp.sum(hidden.astype(f32) * hg, axis=1, keepdims=True)

    @pl.when(step == 0)
    def _():
        dots_ref[...] = dots

    @pl.when(step > 0)
    def _():
        dots_ref[...] += dots

    owners = sums_ref.shape[0]
    rows = xt_ref.shape[0] // owners
    xt = xt_ref[...]
    for k in range(2):
        joint_ref[k] = joint[k]
        part = jnp.dot(xt, joint[k], preferred_element_type=f32)
        for r in range(owners):
            piece = part[rows * r : rows * (r + 1), :] * gu_scale[rows * r // QBLOCK, k]
            for c in range(FTILE // LANES):
                at = (2 * k + c) * rows
                sums_ref[r, at : at + rows, :] = piece[:, LANES * c : LANES * (c + 1)].astype(bf16)
    part = lax.dot_general(
        hidden, g_ref[...], (((0,), (0,)), ((), ())), preferred_element_type=f32
    )
    drows = FTILE // owners
    base = 2 * (FTILE // LANES) * rows
    for r in range(owners):
        own = (r % 2) * (owners // 2) + r // 2
        piece = part[drows * own : drows * (own + 1), :] * d_scale[
            step * (FTILE // QBLOCK) + drows * own // QBLOCK
        ]
        early_ref[drows * own : drows * (own + 1), :] = piece[:, : LANES * EARLY].astype(bf16)
        for c in range(EARLY, part.shape[1] // LANES):
            at = base + (c - EARLY) * drows
            sums_ref[r, at : at + drows, :] = piece[:, LANES * c : LANES * (c + 1)].astype(bf16)


def hidden_step(gu_scale, d_scale, x, xt, g, hg, weights, owners):
    slots, width = x.shape
    hidden = hg.shape[1]
    steps = hidden // FTILE
    rows = width // owners
    per_step = 2 * (FTILE // LANES) * rows + (FTILE // owners) * (width // LANES - EARLY)
    smem = pl.BlockSpec(memory_space=pltpu.SMEM)
    whole = lambda a: pl.BlockSpec(a.shape, lambda i: (0, 0))
    flops = 2 * slots * width * hidden * 5
    return pl.pallas_call(
        hidden_kernel,
        grid=(steps,),
        in_specs=[
            smem,
            smem,
            whole(x),
            whole(xt),
            whole(g),
            pl.BlockSpec((slots, FTILE), lambda i: (0, i)),
            pl.BlockSpec((width, FTILE), lambda i: (0, i)),
            pl.BlockSpec((width, FTILE), lambda i, n=steps: (0, n + i)),
        ],
        out_specs=[
            pl.BlockSpec((owners, per_step, LANES), lambda i: (0, i, 0)),
            pl.BlockSpec((FTILE, LANES * EARLY), lambda i: (i, 0)),
            pl.BlockSpec((2, slots, FTILE), lambda i: (0, 0, i)),
            pl.BlockSpec((slots, 1), lambda i: (0, 0)),
        ],
        out_shape=[
            jax.ShapeDtypeStruct((owners, per_step * steps, LANES), bf16),
            jax.ShapeDtypeStruct((hidden, LANES * EARLY), bf16),
            jax.ShapeDtypeStruct((2, slots, hidden), bf16),
            jax.ShapeDtypeStruct((slots, 1), f32),
        ],
        compiler_params=pltpu.CompilerParams(vmem_limit_bytes=60 * 1024 * 1024),
        cost_estimate=pl.CostEstimate(
            flops=flops, bytes_accessed=14 * 1024 * 1024, transcendentals=slots * hidden
        ),
    )(gu_scale, d_scale, x, xt, g, hg, weights, weights)


def rows_kernel(gu_scale, joint_ref, dots_ref, wg_ref, wu_ref, out_ref, total):
    step = pl.program_id(0)
    contract = (((1,), (1,)), ((), ()))
    part = lax.dot_general(
        joint_ref[0], scaled_rows(wg_ref, gu_scale, 0), contract, preferred_element_type=f32
    ) + lax.dot_general(
        joint_ref[1], scaled_rows(wu_ref, gu_scale, 1), contract, preferred_element_type=f32
    )

    @pl.when(step == 0)
    def _():
        total[...] = part

    @pl.when(step > 0)
    def _():
        total[...] += part

    @pl.when(step == pl.num_programs(0) - 1)
    def _():
        width = total.shape[1]
        out_ref[:, :width] = total[...].astype(bf16)
        dots = dots_ref[...]
        high = dots.astype(bf16).astype(f32)
        lane = lax.broadcasted_iota(jnp.int32, (dots.shape[0], LANES), 1)
        out_ref[:, width:] = jnp.where(
            lane == 0, high, jnp.where(lane == 1, dots - high, 0.0)
        ).astype(bf16)


def rows_step(gu_scale, joint, dots, weights):
    slots, hidden = joint.shape[1:]
    width = weights.shape[0]
    steps = hidden // FTILE
    return pl.pallas_call(
        rows_kernel,
        grid=(steps,),
        in_specs=[
            pl.BlockSpec(memory_space=pltpu.SMEM),
            pl.BlockSpec((2, slots, FTILE), lambda i: (0, 0, i)),
            pl.BlockSpec((slots, 1), lambda i: (0, 0)),
            pl.BlockSpec((width, FTILE), lambda i: (0, i)),
            pl.BlockSpec((width, FTILE), lambda i, n=steps: (0, n + i)),
        ],
        out_specs=pl.BlockSpec((slots, width + LANES), lambda i: (0, 0)),
        out_shape=jax.ShapeDtypeStruct((slots, width + LANES), bf16),
        scratch_shapes=[pltpu.VMEM((slots, width), f32)],
        compiler_params=pltpu.CompilerParams(vmem_limit_bytes=32 * 1024 * 1024),
        cost_estimate=pl.CostEstimate(
            flops=4 * slots * width * hidden, bytes_accessed=6 * 1024 * 1024, transcendentals=0
        ),
    )(gu_scale, joint, dots, weights, weights)


def body(
    tokens,
    grad_out,
    expert_ids,
    route_probs,
    gate_up_weight,
    down_weight,
    gate_up_scale_index,
    down_scale_index,
    scale_table,
):
    groups = lax.axis_size("expert")
    owners = lax.axis_size("dp")
    tok_dev, width = tokens.shape
    hidden = down_weight.shape[1]
    capacity = 4 * tok_dev // groups
    slots = groups * capacity
    steps = hidden // FTILE

    gathered = lax.all_gather(
        gate_up_weight.reshape(gate_up_weight.shape[0], 2 * hidden), "dp", axis=0, tiled=True
    )

    slot_hits = slot_tables(expert_ids, groups, capacity)
    either = (slot_hits[:, 0] + slot_hits[:, 1]).astype(bf16)
    weighing = jnp.sum(slot_hits * route_probs.astype(f32)[:, :, None], axis=1).astype(bf16)
    pack = lambda table, values: (
        jnp.einsum("ts,td->sd", table, values, preferred_element_type=f32)
        .astype(bf16)
        .reshape(groups, capacity, width)
    )
    send = jnp.concatenate([pack(either, tokens), pack(weighing, grad_out)], axis=1)
    recv = lax.all_to_all(send, "expert", split_axis=0, concat_axis=0, tiled=True)
    x = recv[:, :capacity].reshape(slots, width)
    g = recv[:, capacity:].reshape(slots, width)
    xt = x.T
    gu_scale = lookup(gate_up_scale_index[:, 0, :], scale_table)
    d_scale = lookup(down_scale_index[0], scale_table)
    down_eff = (
        down_weight[0].astype(f32) * jnp.repeat(d_scale, QBLOCK)[:, None]
    ).astype(bf16)
    hg = jnp.einsum("sd,fd->sf", g, down_eff, preferred_element_type=f32)

    sums, early, joint, dots = hidden_step(gu_scale, d_scale, x, xt, g, hg, gathered, owners)
    mine = lax.psum_scatter(sums, "dp", scatter_dimension=0, tiled=True)
    parts = lax.all_to_all(
        early.reshape(owners, hidden // owners, LANES * EARLY),
        "dp",
        split_axis=0,
        concat_axis=0,
        tiled=True,
    )
    row_grads = rows_step(gu_scale, joint, dots, gathered)
    row_grads, parts = lax.optimization_barrier((row_grads, parts))
    back = lax.all_to_all(
        row_grads.reshape(groups, capacity, width + LANES),
        "expert",
        split_axis=0,
        concat_axis=0,
        tiled=True,
    ).reshape(slots, width + LANES)
    down_early = lax.all_gather(
        jnp.sum(parts.astype(f32), axis=0).astype(bf16), "dp", axis=0, tiled=True
    )
    token_grad = jnp.dot(either, back[:, :width], preferred_element_type=f32).astype(bf16)
    picked = jnp.einsum(
        "tks,sl->tkl", slot_hits.astype(bf16), back[:, width:], preferred_element_type=f32
    )
    prob_grad = jnp.sum(picked, axis=-1) / route_probs.astype(f32)

    mine, down_early, token_grad, prob_grad = lax.optimization_barrier(
        (mine, down_early, token_grad, prob_grad)
    )
    rows = width // owners
    tiles = FTILE // LANES
    mine = mine.reshape(steps, -1, LANES)
    cut = 2 * tiles * rows
    gate_up_grad = (
        mine[:, :cut]
        .reshape(steps, 2, tiles, rows, LANES)
        .transpose(3, 1, 0, 2, 4)
        .reshape(rows, 1, 2 * hidden)
    )
    drows = FTILE // owners
    late = width - LANES * EARLY
    own = (
        mine[:, cut:]
        .reshape(steps, late // LANES, drows, LANES)
        .transpose(0, 2, 1, 3)
        .reshape(steps, drows, late)
    )
    same_parity = [list(range(k, owners, 2)) for k in range(2)]
    neighbours = [[k, k + 1] for k in range(0, owners, 2)]
    gather = lambda a, sets: lax.all_gather(
        a, "dp", axis=1, tiled=True, axis_index_groups=sets
    )
    down_late = gather(gather(own, same_parity), neighbours).reshape(hidden, late)
    down_grad = jnp.concatenate([down_early, down_late], axis=1)[None]
    return (token_grad, prob_grad, gate_up_grad, down_grad)


def solution(mesh):
    in_specs = (
        P(("dp", "expert"), None),
        P(("dp", "expert"), None),
        P(("dp", "expert"), None),
        P(("dp", "expert"), None),
        P("dp", "expert", None),
        P("expert", None, None),
        P(None, "expert", None),
        P("expert", None),
        P(),
    )
    out_specs = (
        P(("dp", "expert"), None),
        P(("dp", "expert"), None),
        P("dp", "expert", None),
        P("expert", None, None),
    )
    return jax.shard_map(body, mesh=mesh, in_specs=in_specs, out_specs=out_specs, check_vma=False)
```

```python
import jax
import jax.numpy as jnp
from jax import lax
from jax.experimental import pallas as pl
from jax.experimental.pallas import tpu as pltpu
from jax.sharding import PartitionSpec as P

QBLOCK = 128
LANES = 128
FTILE = 256
EARLY = 3
bf16 = jnp.bfloat16
f32 = jnp.float32


def lookup(level_index, level_table):
    onehot = (level_index[..., None] == jnp.arange(level_table.shape[0], dtype=jnp.int32)).astype(
        level_table.dtype
    )
    return jnp.sum(onehot * level_table, axis=-1)


def slot_tables(routes, experts, capacity):
    flat_routes = routes.reshape(-1)
    expert_hits = (flat_routes[:, None] == jnp.arange(experts, dtype=jnp.int32)[None, :]).astype(
        jnp.int32
    )
    place = jnp.arange(flat_routes.shape[0], dtype=jnp.int32)
    earlier = (place[None, :] < place[:, None]).astype(bf16)
    before = jnp.dot(earlier, expert_hits.astype(bf16), preferred_element_type=f32).astype(
        jnp.int32
    )
    slot_rank = jnp.sum(before * expert_hits, axis=1)
    destination = flat_routes * capacity + slot_rank
    table_hits = destination[:, None] == jnp.arange(experts * capacity, dtype=jnp.int32)[None, :]
    return table_hits.astype(f32).reshape(routes.shape[0], 2, experts * capacity)


def scaled_rows(w_ref, scale_ref, part):
    blocks = w_ref.shape[0] // QBLOCK
    pieces = [
        (w_ref[QBLOCK * b : QBLOCK * (b + 1), :].astype(f32) * scale_ref[b, part]).astype(bf16)
        for b in range(blocks)
    ]
    return jnp.concatenate(pieces, axis=0)


def hidden_kernel(
    gu_scale, d_scale, x_ref, xt_ref, g_ref, hg_ref, wg_ref, wu_ref, sums_ref, early_ref, joint_ref, dots_ref
):
    step = pl.program_id(0)
    x = x_ref[...]
    gate = jnp.dot(x, scaled_rows(wg_ref, gu_scale, 0), preferred_element_type=f32)
    up = jnp.dot(x, scaled_rows(wu_ref, gu_scale, 1), preferred_element_type=f32)
    sig = jax.nn.sigmoid(gate)
    act = gate * sig
    hidden = (act * up).astype(bf16)
    hg = hg_ref[:, pl.ds(pl.multiple_of(step * FTILE, FTILE), FTILE)]
    joint = (
        (hg * up * sig * (1.0 + gate * (1.0 - sig))).astype(bf16),
        (hg * act).astype(bf16),
    )
    dots = jnp.sum(hidden.astype(f32) * hg, axis=1, keepdims=True)

    @pl.when(step == 0)
    def _():
        dots_ref[...] = dots

    @pl.when(step > 0)
    def _():
        dots_ref[...] += dots

    owners = sums_ref.shape[0]
    rows = xt_ref.shape[0] // owners
    xt = xt_ref[...]
    for k in range(2):
        joint_ref[k] = joint[k]
        part = jnp.dot(xt, joint[k], preferred_element_type=f32)
        for r in range(owners):
            piece = part[rows * r : rows * (r + 1), :] * gu_scale[rows * r // QBLOCK, k]
            for c in range(FTILE // LANES):
                at = (2 * k + c) * rows
                sums_ref[r, at : at + rows, :] = piece[:, LANES * c : LANES * (c + 1)].astype(bf16)
    part = lax.dot_general(
        hidden, g_ref[...], (((0,), (0,)), ((), ())), preferred_element_type=f32
    )
    drows = FTILE // owners
    base = 2 * (FTILE // LANES) * rows
    for r in range(owners):
        piece = part[drows * r : drows * (r + 1), :] * d_scale[
            step * (FTILE // QBLOCK) + drows * r // QBLOCK
        ]
        early_ref[drows * r : drows * (r + 1), :] = piece[:, : LANES * EARLY].astype(bf16)
        for c in range(EARLY, part.shape[1] // LANES):
            at = base + (c - EARLY) * drows
            sums_ref[r, at : at + drows, :] = piece[:, LANES * c : LANES * (c + 1)].astype(bf16)


def hidden_step(gu_scale, d_scale, x, xt, g, hg, weights, owners):
    slots, width = x.shape
    hidden = hg.shape[1]
    steps = hidden // FTILE
    rows = width // owners
    per_step = 2 * (FTILE // LANES) * rows + (FTILE // owners) * (width // LANES - EARLY)
    smem = pl.BlockSpec(memory_space=pltpu.SMEM)
    vmem = pl.BlockSpec(memory_space=pltpu.VMEM)
    flops = 2 * slots * width * hidden * 5
    return pl.pallas_call(
        hidden_kernel,
        grid=(steps,),
        in_specs=[
            smem,
            smem,
            vmem,
            vmem,
            vmem,
            vmem,
            pl.BlockSpec((width, FTILE), lambda i: (0, i)),
            pl.BlockSpec((width, FTILE), lambda i, n=steps: (0, n + i)),
        ],
        out_specs=[
            pl.BlockSpec((owners, per_step, LANES), lambda i: (0, i, 0)),
            pl.BlockSpec((FTILE, LANES * EARLY), lambda i: (i, 0)),
            pl.BlockSpec((2, slots, FTILE), lambda i: (0, 0, i)),
            pl.BlockSpec((slots, 1), lambda i: (0, 0)),
        ],
        out_shape=[
            pltpu.HBM((owners, per_step * steps, LANES), bf16),
            pltpu.HBM((hidden, LANES * EARLY), bf16),
            pltpu.HBM((2, slots, hidden), bf16),
            pltpu.HBM((slots, 1), f32),
        ],
        compiler_params=pltpu.CompilerParams(vmem_limit_bytes=48 * 1024 * 1024),
        cost_estimate=pl.CostEstimate(
            flops=flops, bytes_accessed=14 * 1024 * 1024, transcendentals=slots * hidden
        ),
    )(gu_scale, d_scale, x, xt, g, hg, weights, weights)


def rows_kernel(gu_scale, joint_ref, dots_ref, wg_ref, wu_ref, out_ref, total):
    step = pl.program_id(0)
    contract = (((1,), (1,)), ((), ()))
    part = lax.dot_general(
        joint_ref[0], scaled_rows(wg_ref, gu_scale, 0), contract, preferred_element_type=f32
    ) + lax.dot_general(
        joint_ref[1], scaled_rows(wu_ref, gu_scale, 1), contract, preferred_element_type=f32
    )

    @pl.when(step == 0)
    def _():
        total[...] = part

    @pl.when(step > 0)
    def _():
        total[...] += part

    @pl.when(step == pl.num_programs(0) - 1)
    def _():
        width = total.shape[1]
        out_ref[:, :width] = total[...].astype(bf16)
        dots = dots_ref[...]
        high = dots.astype(bf16).astype(f32)
        lane = lax.broadcasted_iota(jnp.int32, (dots.shape[0], LANES), 1)
        out_ref[:, width:] = jnp.where(
            lane == 0, high, jnp.where(lane == 1, dots - high, 0.0)
        ).astype(bf16)


def rows_step(gu_scale, joint, dots, weights):
    slots, hidden = joint.shape[1:]
    width = weights.shape[0]
    steps = hidden // FTILE
    return pl.pallas_call(
        rows_kernel,
        grid=(steps,),
        in_specs=[
            pl.BlockSpec(memory_space=pltpu.SMEM),
            pl.BlockSpec((2, slots, FTILE), lambda i: (0, 0, i)),
            pl.BlockSpec((slots, 1), lambda i: (0, 0)),
            pl.BlockSpec((width, FTILE), lambda i: (0, i)),
            pl.BlockSpec((width, FTILE), lambda i, n=steps: (0, n + i)),
        ],
        out_specs=pl.BlockSpec((slots, width + LANES), lambda i: (0, 0)),
        out_shape=jax.ShapeDtypeStruct((slots, width + LANES), bf16),
        scratch_shapes=[pltpu.VMEM((slots, width), f32)],
        compiler_params=pltpu.CompilerParams(vmem_limit_bytes=32 * 1024 * 1024),
        cost_estimate=pl.CostEstimate(
            flops=4 * slots * width * hidden, bytes_accessed=6 * 1024 * 1024, transcendentals=0
        ),
    )(gu_scale, joint, dots, weights, weights)


def body(
    tokens,
    grad_out,
    expert_ids,
    route_probs,
    gate_up_weight,
    down_weight,
    gate_up_scale_index,
    down_scale_index,
    scale_table,
):
    groups = lax.axis_size("expert")
    owners = lax.axis_size("dp")
    tok_dev, width = tokens.shape
    hidden = down_weight.shape[1]
    capacity = 4 * tok_dev // groups
    slots = groups * capacity
    steps = hidden // FTILE

    gathered = lax.all_gather(
        gate_up_weight.reshape(gate_up_weight.shape[0], 2 * hidden), "dp", axis=0, tiled=True
    )

    slot_hits = slot_tables(expert_ids, groups, capacity)
    either = (slot_hits[:, 0] + slot_hits[:, 1]).astype(bf16)
    weighing = jnp.sum(slot_hits * route_probs.astype(f32)[:, :, None], axis=1).astype(bf16)
    pack = lambda table, values: (
        jnp.einsum("ts,td->sd", table, values, preferred_element_type=f32)
        .astype(bf16)
        .reshape(groups, capacity, width)
    )
    send = jnp.concatenate([pack(either, tokens), pack(weighing, grad_out)], axis=1)
    recv = lax.all_to_all(send, "expert", split_axis=0, concat_axis=0, tiled=True)
    x = recv[:, :capacity].reshape(slots, width)
    g = recv[:, capacity:].reshape(slots, width)
    xt = x.T
    gu_scale = lookup(gate_up_scale_index[:, 0, :], scale_table)
    d_scale = lookup(down_scale_index[0], scale_table)
    down_eff = (
        down_weight[0].astype(f32) * jnp.repeat(d_scale, QBLOCK)[:, None]
    ).astype(bf16)
    hg = jnp.einsum("sd,fd->sf", g, down_eff, preferred_element_type=f32)

    sums, early, joint, dots = hidden_step(gu_scale, d_scale, x, xt, g, hg, gathered, owners)
    mine = lax.psum_scatter(sums, "dp", scatter_dimension=0, tiled=True)
    parts = lax.all_to_all(
        early.reshape(owners, hidden // owners, LANES * EARLY),
        "dp",
        split_axis=0,
        concat_axis=0,
        tiled=True,
    )
    row_grads = rows_step(gu_scale, joint, dots, gathered)
    row_grads, parts = lax.optimization_barrier((row_grads, parts))
    back = lax.all_to_all(
        row_grads.reshape(groups, capacity, width + LANES),
        "expert",
        split_axis=0,
        concat_axis=0,
        tiled=True,
    ).reshape(slots, width + LANES)
    down_early = lax.all_gather(
        jnp.sum(parts.astype(f32), axis=0).astype(bf16), "dp", axis=0, tiled=True
    )
    token_grad = jnp.dot(either, back[:, :width], preferred_element_type=f32).astype(bf16)
    picked = jnp.einsum(
        "tks,sl->tkl", slot_hits.astype(bf16), back[:, width:], preferred_element_type=f32
    )
    prob_grad = jnp.sum(picked, axis=-1) / route_probs.astype(f32)

    mine, down_early, token_grad, prob_grad = lax.optimization_barrier(
        (mine, down_early, token_grad, prob_grad)
    )
    rows = width // owners
    tiles = FTILE // LANES
    mine = mine.reshape(steps, -1, LANES)
    cut = 2 * tiles * rows
    gate_up_grad = (
        mine[:, :cut]
        .reshape(steps, 2, tiles, rows, LANES)
        .transpose(3, 1, 0, 2, 4)
        .reshape(rows, 1, 2 * hidden)
    )
    drows = FTILE // owners
    late = width - LANES * EARLY
    late = width - LANES * EARLY
    own = (
        mine[:, cut:]
        .reshape(steps, late // LANES, drows, LANES)
        .transpose(0, 2, 1, 3)
        .reshape(steps, drows, late)
    )
    down_late = lax.all_gather(own, "dp", axis=1, tiled=True).reshape(hidden, late)
    down_grad = jnp.concatenate([down_early, down_late], axis=1)[None]
    return (token_grad, prob_grad, gate_up_grad, down_grad)


def solution(mesh):
    in_specs = (
        P(("dp", "expert"), None),
        P(("dp", "expert"), None),
        P(("dp", "expert"), None),
        P(("dp", "expert"), None),
        P("dp", "expert", None),
        P("expert", None, None),
        P(None, "expert", None),
        P("expert", None),
        P(),
    )
    out_specs = (
        P(("dp", "expert"), None),
        P(("dp", "expert"), None),
        P("dp", "expert", None),
        P("expert", None, None),
    )
    return jax.shard_map(body, mesh=mesh, in_specs=in_specs, out_specs=out_specs, check_vma=False)
```

```python
import functools

import jax
import jax.numpy as jnp
from jax import lax
from jax.experimental import pallas as pl
from jax.experimental.pallas import tpu as pltpu
from jax.sharding import PartitionSpec as P

QBLOCK = 128
LANES = 128
FTILE = 256
EARLY = 3
bf16 = jnp.bfloat16
f32 = jnp.float32


def lookup(level_index, level_table):
    onehot = (level_index[..., None] == jnp.arange(level_table.shape[0], dtype=jnp.int32)).astype(
        level_table.dtype
    )
    return jnp.sum(onehot * level_table, axis=-1)


def slot_tables(routes, experts, capacity):
    flat_routes = routes.reshape(-1)
    expert_hits = (flat_routes[:, None] == jnp.arange(experts, dtype=jnp.int32)[None, :]).astype(
        jnp.int32
    )
    place = jnp.arange(flat_routes.shape[0], dtype=jnp.int32)
    earlier = (place[None, :] < place[:, None]).astype(bf16)
    before = jnp.dot(earlier, expert_hits.astype(bf16), preferred_element_type=f32).astype(
        jnp.int32
    )
    slot_rank = jnp.sum(before * expert_hits, axis=1)
    destination = flat_routes * capacity + slot_rank
    table_hits = destination[:, None] == jnp.arange(experts * capacity, dtype=jnp.int32)[None, :]
    return table_hits.astype(f32).reshape(routes.shape[0], 2, experts * capacity)


def scaled_rows(w_ref, scale_ref, part):
    blocks = w_ref.shape[0] // QBLOCK
    pieces = [
        (w_ref[QBLOCK * b : QBLOCK * (b + 1), :].astype(f32) * scale_ref[b, part]).astype(bf16)
        for b in range(blocks)
    ]
    return jnp.concatenate(pieces, axis=0)


def hidden_kernel(
    gu_scale, d_scale, x_ref, xt_ref, g_ref, hg_ref, wg_ref, wu_ref, sums_ref, early_ref, joint_ref, dots_ref
):
    step = pl.program_id(0)
    x = x_ref[...]
    gate = jnp.dot(x, scaled_rows(wg_ref, gu_scale, 0), preferred_element_type=f32)
    up = jnp.dot(x, scaled_rows(wu_ref, gu_scale, 1), preferred_element_type=f32)
    sig = jax.nn.sigmoid(gate)
    act = gate * sig
    hidden = (act * up).astype(bf16)
    hg = hg_ref[...]
    joint = (
        (hg * up * sig * (1.0 + gate * (1.0 - sig))).astype(bf16),
        (hg * act).astype(bf16),
    )
    dots = jnp.sum(hidden.astype(f32) * hg, axis=1, keepdims=True)

    @pl.when(step == 0)
    def _():
        dots_ref[...] = dots

    @pl.when(step > 0)
    def _():
        dots_ref[...] += dots

    owners = sums_ref.shape[0]
    rows = xt_ref.shape[0] // owners
    xt = xt_ref[...]
    for k in range(2):
        joint_ref[k] = joint[k]
        part = jnp.dot(xt, joint[k], preferred_element_type=f32)
        for r in range(owners):
            piece = part[rows * r : rows * (r + 1), :] * gu_scale[rows * r // QBLOCK, k]
            for c in range(FTILE // LANES):
                at = (2 * k + c) * rows
                sums_ref[r, at : at + rows, :] = piece[:, LANES * c : LANES * (c + 1)].astype(bf16)
    part = lax.dot_general(
        hidden, g_ref[...], (((0,), (0,)), ((), ())), preferred_element_type=f32
    )
    drows = FTILE // owners
    base = 2 * (FTILE // LANES) * rows
    for r in range(owners):
        piece = part[drows * r : drows * (r + 1), :] * d_scale[
            step * (FTILE // QBLOCK) + drows * r // QBLOCK
        ]
        early_ref[drows * r : drows * (r + 1), :] = piece[:, : LANES * EARLY].astype(bf16)
        for c in range(EARLY, part.shape[1] // LANES):
            at = base + (c - EARLY) * drows
            sums_ref[r, at : at + drows, :] = piece[:, LANES * c : LANES * (c + 1)].astype(bf16)


def hidden_step(gu_scale, d_scale, x, xt, g, hg, weights, owners):
    slots, width = x.shape
    hidden = hg.shape[1]
    steps = hidden // FTILE
    rows = width // owners
    per_step = 2 * (FTILE // LANES) * rows + (FTILE // owners) * (width // LANES - EARLY)
    smem = pl.BlockSpec(memory_space=pltpu.SMEM)
    vmem = pl.BlockSpec(memory_space=pltpu.VMEM)
    flops = 2 * slots * width * hidden * 5
    return pl.pallas_call(
        hidden_kernel,
        grid=(steps,),
        in_specs=[
            smem,
            smem,
            vmem,
            vmem,
            vmem,
            pl.BlockSpec((slots, FTILE), lambda i: (0, i)),
            pl.BlockSpec((width, FTILE), lambda i: (0, i)),
            pl.BlockSpec((width, FTILE), lambda i, n=steps: (0, n + i)),
        ],
        out_specs=[
            pl.BlockSpec((owners, per_step, LANES), lambda i: (0, i, 0)),
            pl.BlockSpec((FTILE, LANES * EARLY), lambda i: (i, 0)),
            pl.BlockSpec((2, slots, FTILE), lambda i: (0, 0, i)),
            pl.BlockSpec((slots, 1), lambda i: (0, 0)),
        ],
        out_shape=[
            pltpu.HBM((owners, per_step * steps, LANES), bf16),
            pltpu.HBM((hidden, LANES * EARLY), bf16),
            pltpu.HBM((2, slots, hidden), bf16),
            pltpu.HBM((slots, 1), f32),
        ],
        compiler_params=pltpu.CompilerParams(vmem_limit_bytes=48 * 1024 * 1024),
        cost_estimate=pl.CostEstimate(
            flops=flops, bytes_accessed=14 * 1024 * 1024, transcendentals=slots * hidden
        ),
    )(gu_scale, d_scale, x, xt, g, pltpu.with_memory_space_constraint(hg, pltpu.HBM), weights, weights)


def rows_kernel(gu_scale, joint_ref, dots_ref, wg_ref, wu_ref, out_ref, total):
    step = pl.program_id(0)
    contract = (((1,), (1,)), ((), ()))
    part = lax.dot_general(
        joint_ref[0], scaled_rows(wg_ref, gu_scale, 0), contract, preferred_element_type=f32
    ) + lax.dot_general(
        joint_ref[1], scaled_rows(wu_ref, gu_scale, 1), contract, preferred_element_type=f32
    )

    @pl.when(step == 0)
    def _():
        total[...] = part

    @pl.when(step > 0)
    def _():
        total[...] += part

    @pl.when(step == pl.num_programs(0) - 1)
    def _():
        width = total.shape[1]
        out_ref[:, :width] = total[...].astype(bf16)
        dots = dots_ref[...]
        high = dots.astype(bf16).astype(f32)
        lane = lax.broadcasted_iota(jnp.int32, (dots.shape[0], LANES), 1)
        out_ref[:, width:] = jnp.where(
            lane == 0, high, jnp.where(lane == 1, dots - high, 0.0)
        ).astype(bf16)


def rows_step(gu_scale, joint, dots, weights):
    slots, hidden = joint.shape[1:]
    width = weights.shape[0]
    steps = hidden // FTILE
    return pl.pallas_call(
        rows_kernel,
        grid=(steps,),
        in_specs=[
            pl.BlockSpec(memory_space=pltpu.SMEM),
            pl.BlockSpec((2, slots, FTILE), lambda i: (0, 0, i)),
            pl.BlockSpec((slots, 1), lambda i: (0, 0)),
            pl.BlockSpec((width, FTILE), lambda i: (0, i)),
            pl.BlockSpec((width, FTILE), lambda i, n=steps: (0, n + i)),
        ],
        out_specs=pl.BlockSpec((slots, width + LANES), lambda i: (0, 0)),
        out_shape=jax.ShapeDtypeStruct((slots, width + LANES), bf16),
        scratch_shapes=[pltpu.VMEM((slots, width), f32)],
        compiler_params=pltpu.CompilerParams(vmem_limit_bytes=32 * 1024 * 1024),
        cost_estimate=pl.CostEstimate(
            flops=4 * slots * width * hidden, bytes_accessed=6 * 1024 * 1024, transcendentals=0
        ),
    )(gu_scale, joint, dots, weights, weights)


def layout_kernel(hidden, mine_ref, gate_up_ref, own_ref):
    rows = gate_up_ref.shape[0]
    steps, drows, late = own_ref.shape
    tiles = FTILE // LANES
    for i in range(steps):
        for k in range(2):
            for c in range(tiles):
                at = (tiles * k + c) * rows
                to = hidden * k + FTILE * i + LANES * c
                gate_up_ref[:, to : to + LANES] = mine_ref[i, at : at + rows, :]
        for c in range(late // LANES):
            at = 2 * tiles * rows + c * drows
            own_ref[i, :, LANES * c : LANES * (c + 1)] = mine_ref[i, at : at + drows, :]


def layout_step(mine, hidden, rows, drows, late):
    steps = mine.shape[0]
    return pl.pallas_call(
        functools.partial(layout_kernel, hidden),
        out_shape=[
            jax.ShapeDtypeStruct((rows, 2 * hidden), bf16),
            jax.ShapeDtypeStruct((steps, drows, late), bf16),
        ],
        cost_estimate=pl.CostEstimate(flops=0, bytes_accessed=1024 * 1024, transcendentals=0),
    )(mine)


def body(
    tokens,
    grad_out,
    expert_ids,
    route_probs,
    gate_up_weight,
    down_weight,
    gate_up_scale_index,
    down_scale_index,
    scale_table,
):
    groups = lax.axis_size("expert")
    owners = lax.axis_size("dp")
    tok_dev, width = tokens.shape
    hidden = down_weight.shape[1]
    capacity = 4 * tok_dev // groups
    slots = groups * capacity
    steps = hidden // FTILE

    gathered = lax.all_gather(
        gate_up_weight.reshape(gate_up_weight.shape[0], 2 * hidden), "dp", axis=0, tiled=True
    )

    slot_hits = slot_tables(expert_ids, groups, capacity)
    either = (slot_hits[:, 0] + slot_hits[:, 1]).astype(bf16)
    weighing = jnp.sum(slot_hits * route_probs.astype(f32)[:, :, None], axis=1).astype(bf16)
    pack = lambda table, values: (
        jnp.einsum("ts,td->sd", table, values, preferred_element_type=f32)
        .astype(bf16)
        .reshape(groups, capacity, width)
    )
    send = jnp.concatenate([pack(either, tokens), pack(weighing, grad_out)], axis=1)
    recv = lax.all_to_all(send, "expert", split_axis=0, concat_axis=0, tiled=True)
    x = recv[:, :capacity].reshape(slots, width)
    g = recv[:, capacity:].reshape(slots, width)
    xt = x.T
    gu_scale = lookup(gate_up_scale_index[:, 0, :], scale_table)
    d_scale = lookup(down_scale_index[0], scale_table)
    down_eff = (
        down_weight[0].astype(f32) * jnp.repeat(d_scale, QBLOCK)[:, None]
    ).astype(bf16)
    hg = jnp.einsum("sd,fd->sf", g, down_eff, preferred_element_type=f32)

    sums, early, joint, dots = hidden_step(gu_scale, d_scale, x, xt, g, hg, gathered, owners)
    mine = lax.psum_scatter(sums, "dp", scatter_dimension=0, tiled=True)
    parts = lax.all_to_all(
        early.reshape(owners, hidden // owners, LANES * EARLY),
        "dp",
        split_axis=0,
        concat_axis=0,
        tiled=True,
    )
    row_grads = rows_step(gu_scale, joint, dots, gathered)
    row_grads, parts = lax.optimization_barrier((row_grads, parts))
    back = lax.all_to_all(
        row_grads.reshape(groups, capacity, width + LANES),
        "expert",
        split_axis=0,
        concat_axis=0,
        tiled=True,
    ).reshape(slots, width + LANES)
    down_early = lax.all_gather(
        jnp.sum(parts.astype(f32), axis=0).astype(bf16), "dp", axis=0, tiled=True
    )
    token_grad = jnp.dot(either, back[:, :width], preferred_element_type=f32).astype(bf16)
    picked = jnp.einsum(
        "tks,sl->tkl", slot_hits.astype(bf16), back[:, width:], preferred_element_type=f32
    )
    prob_grad = jnp.sum(picked, axis=-1) / route_probs.astype(f32)

    mine, down_early, token_grad, prob_grad = lax.optimization_barrier(
        (mine, down_early, token_grad, prob_grad)
    )
    late = width - LANES * EARLY
    gate_up_grad, own = layout_step(
        mine.reshape(steps, -1, LANES), hidden, width // owners, FTILE // owners, late
    )
    gate_up_grad = gate_up_grad[:, None, :]
    down_late = lax.all_gather(own, "dp", axis=1, tiled=True).reshape(hidden, late)
    down_grad = jnp.concatenate([down_early, down_late], axis=1)[None]
    return (token_grad, prob_grad, gate_up_grad, down_grad)


def solution(mesh):
    in_specs = (
        P(("dp", "expert"), None),
        P(("dp", "expert"), None),
        P(("dp", "expert"), None),
        P(("dp", "expert"), None),
        P("dp", "expert", None),
        P("expert", None, None),
        P(None, "expert", None),
        P("expert", None),
        P(),
    )
    out_specs = (
        P(("dp", "expert"), None),
        P(("dp", "expert"), None),
        P("dp", "expert", None),
        P("expert", None, None),
    )
    return jax.shard_map(body, mesh=mesh, in_specs=in_specs, out_specs=out_specs, check_vma=False)
```

```python
import functools

import jax
import jax.numpy as jnp
from jax import lax
from jax.experimental import pallas as pl
from jax.experimental.pallas import tpu as pltpu
from jax.sharding import PartitionSpec as P

QBLOCK = 128
LANES = 128
FTILE = 256
EARLY = 3
bf16 = jnp.bfloat16
f32 = jnp.float32


def lookup(level_index, level_table):
    onehot = (level_index[..., None] == jnp.arange(level_table.shape[0], dtype=jnp.int32)).astype(
        level_table.dtype
    )
    return jnp.sum(onehot * level_table, axis=-1)


def slot_tables(routes, experts, capacity):
    flat_routes = routes.reshape(-1)
    expert_hits = (flat_routes[:, None] == jnp.arange(experts, dtype=jnp.int32)[None, :]).astype(
        jnp.int32
    )
    place = jnp.arange(flat_routes.shape[0], dtype=jnp.int32)
    earlier = (place[None, :] < place[:, None]).astype(bf16)
    before = jnp.dot(earlier, expert_hits.astype(bf16), preferred_element_type=f32).astype(
        jnp.int32
    )
    slot_rank = jnp.sum(before * expert_hits, axis=1)
    destination = flat_routes * capacity + slot_rank
    table_hits = destination[:, None] == jnp.arange(experts * capacity, dtype=jnp.int32)[None, :]
    return table_hits.astype(f32).reshape(routes.shape[0], 2, experts * capacity)


def scaled_rows(w_ref, scale_ref, part):
    blocks = w_ref.shape[0] // QBLOCK
    pieces = [
        (w_ref[QBLOCK * b : QBLOCK * (b + 1), :].astype(f32) * scale_ref[b, part]).astype(bf16)
        for b in range(blocks)
    ]
    return jnp.concatenate(pieces, axis=0)


def hidden_kernel(
    gu_scale, d_scale, x_ref, xt_ref, g_ref, hg_ref, wg_ref, wu_ref, sums_ref, early_ref, joint_ref, dots_ref
):
    step = pl.program_id(0)
    x = x_ref[...]
    gate = jnp.dot(x, scaled_rows(wg_ref, gu_scale, 0), preferred_element_type=f32)
    up = jnp.dot(x, scaled_rows(wu_ref, gu_scale, 1), preferred_element_type=f32)
    sig = jax.nn.sigmoid(gate)
    act = gate * sig
    hidden = (act * up).astype(bf16)
    hg = hg_ref[...]
    joint = (
        (hg * up * sig * (1.0 + gate * (1.0 - sig))).astype(bf16),
        (hg * act).astype(bf16),
    )
    dots = jnp.sum(hidden.astype(f32) * hg, axis=1, keepdims=True)

    @pl.when(step == 0)
    def _():
        dots_ref[...] = dots

    @pl.when(step > 0)
    def _():
        dots_ref[...] += dots

    owners = sums_ref.shape[0]
    rows = xt_ref.shape[0] // owners
    xt = xt_ref[...]
    for k in range(2):
        joint_ref[k] = joint[k]
        part = jnp.dot(xt, joint[k], preferred_element_type=f32)
        for r in range(owners):
            piece = part[rows * r : rows * (r + 1), :] * gu_scale[rows * r // QBLOCK, k]
            for c in range(FTILE // LANES):
                at = (2 * k + c) * rows
                sums_ref[r, at : at + rows, :] = piece[:, LANES * c : LANES * (c + 1)].astype(bf16)
    part = lax.dot_general(
        hidden, g_ref[...], (((0,), (0,)), ((), ())), preferred_element_type=f32
    )
    drows = FTILE // owners
    base = 2 * (FTILE // LANES) * rows
    for r in range(owners):
        piece = part[drows * r : drows * (r + 1), :] * d_scale[
            step * (FTILE // QBLOCK) + drows * r // QBLOCK
        ]
        early_ref[drows * r : drows * (r + 1), :] = piece[:, : LANES * EARLY].astype(bf16)
        for c in range(EARLY, part.shape[1] // LANES):
            at = base + (c - EARLY) * drows
            sums_ref[r, at : at + drows, :] = piece[:, LANES * c : LANES * (c + 1)].astype(bf16)


def hidden_step(gu_scale, d_scale, x, xt, g, hg, weights, owners):
    slots, width = x.shape
    hidden = hg.shape[1]
    steps = hidden // FTILE
    rows = width // owners
    per_step = 2 * (FTILE // LANES) * rows + (FTILE // owners) * (width // LANES - EARLY)
    smem = pl.BlockSpec(memory_space=pltpu.SMEM)
    vmem = pl.BlockSpec(memory_space=pltpu.VMEM)
    flops = 2 * slots * width * hidden * 5
    return pl.pallas_call(
        hidden_kernel,
        grid=(steps,),
        in_specs=[
            smem,
            smem,
            vmem,
            vmem,
            vmem,
            pl.BlockSpec((slots, FTILE), lambda i: (0, i)),
            pl.BlockSpec((width, FTILE), lambda i: (0, i)),
            pl.BlockSpec((width, FTILE), lambda i, n=steps: (0, n + i)),
        ],
        out_specs=[
            pl.BlockSpec((owners, per_step, LANES), lambda i: (0, i, 0)),
            pl.BlockSpec((FTILE, LANES * EARLY), lambda i: (i, 0)),
            pl.BlockSpec((2, slots, FTILE), lambda i: (0, 0, i)),
            pl.BlockSpec((slots, 1), lambda i: (0, 0)),
        ],
        out_shape=[
            pltpu.HBM((owners, per_step * steps, LANES), bf16),
            pltpu.HBM((hidden, LANES * EARLY), bf16),
            pltpu.HBM((2, slots, hidden), bf16),
            pltpu.HBM((slots, 1), f32),
        ],
        compiler_params=pltpu.CompilerParams(vmem_limit_bytes=48 * 1024 * 1024),
        cost_estimate=pl.CostEstimate(
            flops=flops, bytes_accessed=14 * 1024 * 1024, transcendentals=slots * hidden
        ),
    )(gu_scale, d_scale, x, xt, g, pltpu.with_memory_space_constraint(hg, pltpu.HBM), weights, weights)


def rows_kernel(gu_scale, joint_ref, dots_ref, wg_ref, wu_ref, out_ref, total):
    step = pl.program_id(0)
    contract = (((1,), (1,)), ((), ()))
    part = lax.dot_general(
        joint_ref[0], scaled_rows(wg_ref, gu_scale, 0), contract, preferred_element_type=f32
    ) + lax.dot_general(
        joint_ref[1], scaled_rows(wu_ref, gu_scale, 1), contract, preferred_element_type=f32
    )

    @pl.when(step == 0)
    def _():
        total[...] = part

    @pl.when(step > 0)
    def _():
        total[...] += part

    @pl.when(step == pl.num_programs(0) - 1)
    def _():
        width = total.shape[1]
        out_ref[:, :width] = total[...].astype(bf16)
        dots = dots_ref[...]
        high = dots.astype(bf16).astype(f32)
        lane = lax.broadcasted_iota(jnp.int32, (dots.shape[0], LANES), 1)
        out_ref[:, width:] = jnp.where(
            lane == 0, high, jnp.where(lane == 1, dots - high, 0.0)
        ).astype(bf16)


def rows_step(gu_scale, joint, dots, weights):
    slots, hidden = joint.shape[1:]
    width = weights.shape[0]
    steps = hidden // FTILE
    return pl.pallas_call(
        rows_kernel,
        grid=(steps,),
        in_specs=[
            pl.BlockSpec(memory_space=pltpu.SMEM),
            pl.BlockSpec((2, slots, FTILE), lambda i: (0, 0, i)),
            pl.BlockSpec((slots, 1), lambda i: (0, 0)),
            pl.BlockSpec((width, FTILE), lambda i: (0, i)),
            pl.BlockSpec((width, FTILE), lambda i, n=steps: (0, n + i)),
        ],
        out_specs=pl.BlockSpec((slots, width + LANES), lambda i: (0, 0)),
        out_shape=jax.ShapeDtypeStruct((slots, width + LANES), bf16),
        scratch_shapes=[pltpu.VMEM((slots, width), f32)],
        compiler_params=pltpu.CompilerParams(vmem_limit_bytes=32 * 1024 * 1024),
        cost_estimate=pl.CostEstimate(
            flops=4 * slots * width * hidden, bytes_accessed=6 * 1024 * 1024, transcendentals=0
        ),
    )(gu_scale, joint, dots, weights, weights)


def layout_kernel(hidden, mine_ref, gate_up_ref, own_ref):
    rows = gate_up_ref.shape[0]
    steps, drows, late = own_ref.shape
    tiles = FTILE // LANES
    for i in range(steps):
        for k in range(2):
            for c in range(tiles):
                at = (tiles * k + c) * rows
                to = hidden * k + FTILE * i + LANES * c
                gate_up_ref[:, to : to + LANES] = mine_ref[i, at : at + rows, :]
        for c in range(late // LANES):
            at = 2 * tiles * rows + c * drows
            own_ref[i, :, LANES * c : LANES * (c + 1)] = mine_ref[i, at : at + drows, :]


def layout_step(mine, hidden, rows, drows, late):
    steps = mine.shape[0]
    return pl.pallas_call(
        functools.partial(layout_kernel, hidden),
        out_shape=[
            jax.ShapeDtypeStruct((rows, 2 * hidden), bf16),
            jax.ShapeDtypeStruct((steps, drows, late), bf16),
        ],
        cost_estimate=pl.CostEstimate(flops=0, bytes_accessed=1024 * 1024, transcendentals=0),
    )(mine)


def body(
    tokens,
    grad_out,
    expert_ids,
    route_probs,
    gate_up_weight,
    down_weight,
    gate_up_scale_index,
    down_scale_index,
    scale_table,
):
    groups = lax.axis_size("expert")
    owners = lax.axis_size("dp")
    tok_dev, width = tokens.shape
    hidden = down_weight.shape[1]
    capacity = 4 * tok_dev // groups
    slots = groups * capacity
    steps = hidden // FTILE

    gathered = lax.all_gather(
        gate_up_weight.reshape(gate_up_weight.shape[0], 2 * hidden), "dp", axis=0, tiled=True
    )

    slot_hits = slot_tables(expert_ids, groups, capacity)
    either = (slot_hits[:, 0] + slot_hits[:, 1]).astype(bf16)
    weighing = jnp.sum(slot_hits * route_probs.astype(f32)[:, :, None], axis=1).astype(bf16)
    pack = lambda table, values: (
        jnp.einsum("ts,td->sd", table, values, preferred_element_type=f32)
        .astype(bf16)
        .reshape(groups, capacity, width)
    )
    send = jnp.concatenate([pack(either, tokens), pack(weighing, grad_out)], axis=1)
    recv = lax.all_to_all(send, "expert", split_axis=0, concat_axis=0, tiled=True)
    x = recv[:, :capacity].reshape(slots, width)
    g = recv[:, capacity:].reshape(slots, width)
    xt = x.T
    gu_scale = lookup(gate_up_scale_index[:, 0, :], scale_table)
    d_scale = lookup(down_scale_index[0], scale_table)
    down_eff = (
        down_weight[0].astype(f32) * jnp.repeat(d_scale, QBLOCK)[:, None]
    ).astype(bf16)
    hg = jnp.einsum("sd,fd->sf", g, down_eff, preferred_element_type=f32)

    sums, early, joint, dots = hidden_step(gu_scale, d_scale, x, xt, g, hg, gathered, owners)
    mine = lax.psum_scatter(sums, "dp", scatter_dimension=0, tiled=True)
    half = hidden // 2
    parity = lax.axis_index("dp") % 2
    given = lax.ppermute(
        lax.dynamic_slice_in_dim(early, (1 - parity) * half, half, axis=0),
        "dp",
        [(z, z + 1 - 2 * (z % 2)) for z in range(owners)],
    )
    kept = lax.dynamic_slice_in_dim(early, parity * half, half, axis=0)
    same_parity = [list(range(k, owners, 2)) for k in range(2)]
    parts = lax.all_to_all(
        (kept.astype(f32) + given.astype(f32))
        .astype(bf16)
        .reshape(owners // 2, hidden // owners, LANES * EARLY),
        "dp",
        split_axis=0,
        concat_axis=0,
        tiled=True,
        axis_index_groups=same_parity,
    )
    row_grads = rows_step(gu_scale, joint, dots, gathered)
    row_grads, parts = lax.optimization_barrier((row_grads, parts))
    back = lax.all_to_all(
        row_grads.reshape(groups, capacity, width + LANES),
        "expert",
        split_axis=0,
        concat_axis=0,
        tiled=True,
    ).reshape(slots, width + LANES)
    down_early = lax.all_gather(
        jnp.sum(parts.astype(f32), axis=0).astype(bf16),
        "dp",
        axis=0,
        tiled=True,
        axis_index_groups=[same_parity[0] + same_parity[1]],
    )
    token_grad = jnp.dot(either, back[:, :width], preferred_element_type=f32).astype(bf16)
    picked = jnp.einsum(
        "tks,sl->tkl", slot_hits.astype(bf16), back[:, width:], preferred_element_type=f32
    )
    prob_grad = jnp.sum(picked, axis=-1) / route_probs.astype(f32)

    mine, down_early, token_grad, prob_grad = lax.optimization_barrier(
        (mine, down_early, token_grad, prob_grad)
    )
    late = width - LANES * EARLY
    gate_up_grad, own = layout_step(
        mine.reshape(steps, -1, LANES), hidden, width // owners, FTILE // owners, late
    )
    gate_up_grad = gate_up_grad[:, None, :]
    down_late = lax.all_gather(own, "dp", axis=1, tiled=True).reshape(hidden, late)
    down_grad = jnp.concatenate([down_early, down_late], axis=1)[None]
    return (token_grad, prob_grad, gate_up_grad, down_grad)


def solution(mesh):
    in_specs = (
        P(("dp", "expert"), None),
        P(("dp", "expert"), None),
        P(("dp", "expert"), None),
        P(("dp", "expert"), None),
        P("dp", "expert", None),
        P("expert", None, None),
        P(None, "expert", None),
        P("expert", None),
        P(),
    )
    out_specs = (
        P(("dp", "expert"), None),
        P(("dp", "expert"), None),
        P("dp", "expert", None),
        P("expert", None, None),
    )
    return jax.shard_map(body, mesh=mesh, in_specs=in_specs, out_specs=out_specs, check_vma=False)
```
